32 devices in a mesh: rep: 2 (over y), grp: 4 (over z), hid: 4 (over x, core).
Axes of the slice: x: 2, y: 2, z: 4, core: 2. Of those that a mesh axis runs over, the one named last changes fastest.
Arguments:
- tokens: bfloat16 [1024, 2304], P(('rep', 'grp')), parts along dimension 0, may hold values from -6 to 6
- routes: int32 [1024, 2], P(('rep', 'grp')), parts along dimension 0, may hold values from 0 to 3, all different within a row; in each aligned block of 128 rows (0 to 127, 128 to 255, ...) at most 64 rows name the same one
- gates: float32 [1024, 2], P(('rep', 'grp')), parts along dimension 0, may hold values from 0.2 to 1
- grad_out: bfloat16 [1024, 2304], P(('rep', 'grp')), parts along dimension 0, may hold values from -6 to 6
- w_gate: bfloat16 [4, 2304, 6144], P('grp', None, 'hid'), may hold values from -0.125 to 0.125
- w_up: bfloat16 [4, 2304, 6144], P('grp', None, 'hid'), may hold values from -0.125 to 0.125
- w_down: bfloat16 [4, 6144, 2304], P('grp', 'hid'), may hold values from -0.078125 to 0.078125
Outputs:
- mixed: bfloat16 [1024, 2304], P(('rep', 'grp', 'hid')), parts along dimension 0
- grad_tokens: bfloat16 [1024, 2304], P(('rep', 'grp', 'hid')), parts along dimension 0
- grad_gate: bfloat16 [8, 2304, 6144], P(('rep', 'grp'), None, 'hid'), parts along dimension 0
- grad_up: bfloat16 [8, 2304, 6144], P(('rep', 'grp'), None, 'hid'), parts along dimension 0
- grad_down: bfloat16 [8, 6144, 2304], P(('rep', 'grp'), 'hid'), parts along dimension 0
The draws below stay inside these ranges and needn't reach their ends.
There are 2 independent parts, one for each index of `rep`. The reference program is written for one: setup_inputs(seed, part) draws one part's arguments, and reference() takes and returns one part's arrays. A program takes and returns all parts, laid end to end along the dimension named above; an argument that names none is the same for every part. Nothing has to cross between parts.
Inputs may be any that keep to these rules, and one draw needn't show every extreme that they name: `routes`: each row names 2 different experts. In each block of 128 rows no expert is named by more than 64 rows, and some block names one expert exactly 64 times.
All inputs are finite; a program needn't handle non-finite values.
Results may differ from the reference program's by a relative error of at most 0.0058.
Values may be sent and summed in bfloat16 or wider, within the bound.
A program may use at most 128 MiB of HBM per device.

```python
import math
import jax
import jax.numpy as jnp
import numpy as np
from jax import lax

D = 2304
FF = 6144
TOP = 2
TOK_DEV = 128
EXPERTS = 4
TOKENS = 512
CAP = 64
N_GRP = 4


def levels(stream_key, shape, cuts, low, largest):
    gain = 1.0
    for axis_at, shards_of in cuts:
        draws = jax.random.uniform(jax.random.fold_in(jax.random.fold_in(stream_key, 6), axis_at), (shards_of,), jnp.float32, low / len(cuts), largest / len(cuts))
        gain = gain * jnp.repeat(jnp.exp(draws), shape[axis_at] // shards_of).reshape((-1,) + (1,) * (len(shape) - 1 - axis_at))
    return gain


def routed_block(own_key, own, number, rows, number_of, top, bound, skew):
    order = jax.random.permutation(own_key, number_of)
    heavy_load, ordinary = portions_of(number_of, rows * top, bound, skew, True), portions_of(number_of, rows * top, bound, skew, False)
    places = jnp.arange(number_of)

    def named(lengths, turn):
        used = int((lengths > 0).sum())
        fixed = max(1, used // 4)
        shifted = fixed + (places - fixed + turn * (used - fixed)) % max(1, number_of - fixed)
        return jnp.zeros((number_of,), jnp.int32).at[order[jnp.where(places < fixed, places, shifted)]].set(jnp.asarray(lengths, jnp.int32))

    lengths = jnp.where(number % 4 == 0, named(heavy_load, number // 4), named(ordinary, number - number // 4 - 1))
    mixed = jax.random.permutation(jax.random.fold_in(own, 3), number_of)
    donor, taker = mixed[0:number_of // 2 * 2:2], mixed[1:number_of // 2 * 2:2]
    margin = jnp.minimum(lengths[donor] - 1, bound - lengths[taker]) // 2
    margin = jnp.where((donor == order[0]) | (taker == order[0]) | (lengths[taker] == 0), 0, jnp.maximum(margin, 0))
    shifted = jax.random.randint(jax.random.fold_in(own, 4), (number_of // 2,), 0, 1 << 20) % (margin + 1)
    lengths = lengths.at[donor].add(-shifted).at[taker].add(shifted)
    members = jnp.searchsorted(jnp.cumsum(lengths), jnp.arange(rows * top), side="right").astype(jnp.int32)
    listing = members.reshape(top, rows).T
    listing = listing[jax.random.permutation(jax.random.fold_in(own, 1), rows)]
    turn = jax.random.randint(jax.random.fold_in(own, 2), (rows, 1), 0, top)
    return jnp.take_along_axis(listing, (jnp.arange(top)[None, :] + turn) % top, axis=1)


def portions_of(count, total, limit, skew, full):
    loads = [(1 << 20) // math.isqrt(grade ** skew) + 1 for grade in range(1, count + 1)]
    largest = limit if full else min(limit, max(-(-total // count), total * loads[0] // sum(loads)))
    least = 1 if total - largest >= count - 1 else 0
    holding, spare = [largest] + [least] * (count - 1), total - largest - least * (count - 1)
    while spare > 0:
        candidates = [i for i in range(1, count) if holding[i] < largest] or [i for i in range(1, count) if holding[i] < limit]
        mass, budget = sum([loads[i] for i in candidates]), spare
        for i in candidates:
            more = min(limit - holding[i], max(1, budget * loads[i] // mass), spare)
            holding[i] = holding[i] + more
            spare = spare - more
    return np.array(holding)


def bell_draw(rng, extent, spread, limit, split=(), kind=jnp.bfloat16):
    array = spread * jax.random.normal(rng, extent, jnp.float32)
    if split:
        array = array * levels(rng, extent, split, -0.22, 0.18)
    return jnp.clip(array, -limit, limit).astype(kind)


def setup_inputs(seed: int = 0, part: int = 0) -> dict:
    streams_of = jax.random.split(jax.random.key(seed), 8)
    own_keys = jax.random.split(jax.random.fold_in(streams_of[7], part), 8)
    tokens = bell_draw(own_keys[0], (TOKENS, D), 1.0, 6.0, ((0, 4),))
    routes_keys = jax.random.split(jax.random.fold_in(own_keys[1], 1), TOKENS // TOK_DEV)
    routes_turns = jax.random.permutation(jax.random.fold_in(own_keys[1], 3), TOKENS // TOK_DEV)
    routes = jax.vmap(lambda own, number: routed_block(jax.random.fold_in(own_keys[1], 2), own, number, TOK_DEV, EXPERTS, TOP, CAP, 2))(routes_keys, routes_turns).reshape((TOKENS, TOP))
    gates = jnp.clip(0.2 + 0.8 * jax.random.uniform(own_keys[2], (TOKENS, TOP), jnp.float32) ** levels(own_keys[2], (TOKENS, TOP), ((0, 4),), -0.2, 0.2), 0.2, 1.0)
    grad_out = bell_draw(own_keys[3], (TOKENS, D), 1.0, 6.0, ((0, 4),))
    w_gate = bell_draw(streams_of[4], (EXPERTS, D, FF), D ** -0.5, 0.125, ((0, 4), (2, 4)))
    w_up = bell_draw(streams_of[5], (EXPERTS, D, FF), D ** -0.5, 0.125, ((0, 4), (2, 4)))
    w_down = bell_draw(streams_of[6], (EXPERTS, FF, D), FF ** -0.5, 0.078125, ((0, 4), (1, 4)))
    return {"tokens": tokens, "routes": routes, "gates": gates, "grad_out": grad_out, "w_gate": w_gate, "w_up": w_up, "w_down": w_down}


def slot_numbers(route_blocks, expert_count):
    onehot = (route_blocks[..., None] == jnp.arange(expert_count, dtype=jnp.int32)).astype(jnp.int32)
    earlier = jnp.cumsum(onehot, axis=-2) - onehot
    return jnp.sum(earlier * onehot, axis=-1).astype(jnp.int32)


def forward_rows(rows_x, weight_gate, weight_up, weight_down):
    gate_pre = jnp.dot(rows_x, weight_gate, preferred_element_type=jnp.float32)
    up_pre = jnp.dot(rows_x, weight_up, preferred_element_type=jnp.float32)
    sigma_gate = jax.nn.sigmoid(gate_pre)
    silu_gate = gate_pre * sigma_gate
    hidden = (silu_gate * up_pre).astype(jnp.bfloat16)
    expert_out = jnp.dot(hidden, weight_down, preferred_element_type=jnp.float32)
    return gate_pre, up_pre, sigma_gate, silu_gate, hidden, expert_out


def backward_rows(rows_x, rows_c, weight_gate, weight_up, weight_down, saved):
    gate_pre, up_pre, sigma_gate, silu_gate, hidden, expert_out = saved
    grad_hidden = jnp.dot(rows_c, weight_down.T, preferred_element_type=jnp.float32)
    slope = sigma_gate * (1.0 + gate_pre * (1.0 - sigma_gate))
    grad_pre_gate = (grad_hidden * up_pre * slope).astype(jnp.bfloat16)
    grad_pre_up = (grad_hidden * silu_gate).astype(jnp.bfloat16)
    grad_rows = jnp.dot(grad_pre_gate, weight_gate.T, preferred_element_type=jnp.float32)
    grad_rows = grad_rows + jnp.dot(grad_pre_up, weight_up.T, preferred_element_type=jnp.float32)
    grad_wgate = jnp.dot(rows_x.T, grad_pre_gate, preferred_element_type=jnp.float32).astype(jnp.bfloat16)
    grad_wup = jnp.dot(rows_x.T, grad_pre_up, preferred_element_type=jnp.float32).astype(jnp.bfloat16)
    grad_wdown = jnp.dot(hidden.T, rows_c, preferred_element_type=jnp.float32).astype(jnp.bfloat16)
    return grad_rows, grad_wgate, grad_wup, grad_wdown


def reference(tokens, routes, gates, grad_out, w_gate, w_up, w_down):
    sources = N_GRP
    pairs = TOK_DEV * TOP
    flat_routes = routes.reshape(sources, TOK_DEV, TOP).transpose(0, 2, 1).reshape(sources, pairs).astype(jnp.int32)
    slot_index = slot_numbers(flat_routes, EXPERTS)
    source_ids = jnp.broadcast_to(jnp.arange(sources, dtype=jnp.int32)[:, None], (sources, pairs))
    tok_pairs = jnp.broadcast_to(tokens.reshape(sources, 1, TOK_DEV, D), (sources, TOP, TOK_DEV, D)).reshape(sources, pairs, D)
    gate_pairs = gates.reshape(sources, TOK_DEV, TOP).transpose(0, 2, 1)[..., None]
    cot_pairs = (gate_pairs * grad_out.reshape(sources, 1, TOK_DEV, D).astype(jnp.float32)).astype(jnp.bfloat16)
    cot_pairs = cot_pairs.reshape(sources, pairs, D)
    empty = jnp.zeros((EXPERTS, sources, CAP, D), jnp.bfloat16)
    rows_x = empty.at[flat_routes, source_ids, slot_index].set(tok_pairs).reshape(EXPERTS, sources * CAP, D)
    rows_c = empty.at[flat_routes, source_ids, slot_index].set(cot_pairs).reshape(EXPERTS, sources * CAP, D)

    def one_expert(items):
        block_x, block_c, weight_gate, weight_up, weight_down = items
        saved = forward_rows(block_x, weight_gate, weight_up, weight_down)
        grad_rows, grad_wgate, grad_wup, grad_wdown = backward_rows(block_x, block_c, weight_gate, weight_up, weight_down, saved)
        return saved[5], grad_rows, grad_wgate, grad_wup, grad_wdown

    out_rows, grad_rows, grad_gate, grad_up, grad_down = lax.map(one_expert, (rows_x, rows_c, w_gate, w_up, w_down))
    out_rows = out_rows.reshape(EXPERTS, sources, CAP, D)
    grad_rows = grad_rows.reshape(EXPERTS, sources, CAP, D)
    picked_out = out_rows[flat_routes, source_ids, slot_index].reshape(sources, TOP, TOK_DEV, D).transpose(0, 2, 1, 3).reshape(TOKENS, TOP, D)
    picked_grad = grad_rows[flat_routes, source_ids, slot_index].reshape(sources, TOP, TOK_DEV, D).transpose(0, 2, 1, 3).reshape(TOKENS, TOP, D)
    mixed = jnp.sum(gates[..., None] * picked_out, axis=1).astype(jnp.bfloat16)
    grad_tokens = jnp.sum(picked_grad, axis=1).astype(jnp.bfloat16)
    return mixed, grad_tokens, grad_gate, grad_up, grad_down
```

```python
import functools

import jax
import jax.numpy as jnp
from jax import lax
from jax.experimental import pallas as pl
from jax.experimental.pallas import tpu as pltpu
from jax.sharding import PartitionSpec as P

MESH = pl.DeviceIdType.MESH
F32 = jnp.float32
BF16 = jnp.bfloat16


def nn(a, b):
    return jnp.dot(a, b, preferred_element_type=F32)


def nt(a, b):
    return lax.dot_general(a, b, (((1,), (1,)), ((), ())), preferred_element_type=F32)


def layer_kernel(
    groups, quarter, tile,
    tok, routes, gates, gout, wg_any, wu_any, wd_any,
    x_any, c_any, hid_any, gpg_any, gpu_any, mixed_out, gtok_out,
    wg, wu, wd, rows_x, rows_c, send, places, picks, silu, upslope, hidden, gpg, gpu,
    acc, pair_send, pair_recv, x_send, x_recv, z_send, home, out_send, out_full,
    zs, zr, xs, xr, cs, cr, c2s, c2r, x2s, x2r, z2s, z2r, h2s, h2r, os_, or_, wsem, lsem,
):
    rep = lax.axis_index("rep")
    g = lax.axis_index("grp")
    h = lax.axis_index("hid")
    x = h // 2
    c = lax.rem(h, 2)
    over = (1 - x) * 2 + c
    sib = x * 2 + 1 - c
    tokens, width = tok.shape
    hc = width // 2
    gq = groups * quarter
    ff = hidden.shape[1]
    share = tokens // 4
    xcols = pl.ds(pl.multiple_of(x * hc, 128), hc)
    ocols = pl.ds(pl.multiple_of((1 - x) * hc, 128), hc)
    rows = (rows_x, rows_c)

    loads = [
        pltpu.make_async_copy(a, b, wsem.at[i])
        for i, (a, b) in enumerate(((wg_any, wg), (wu_any, wu), (wd_any, wd)))
    ]
    for load in loads:
        load.start()

    def group_of(shift):
        return lax.rem(g + shift + groups, groups)

    def block(half, group):
        return pl.ds(pl.multiple_of(half * gq + group * quarter, 16), quarter)

    def remote(src, dst, s_sem, r_sem, grp, hid):
        return pltpu.make_async_remote_copy(
            src_ref=src, dst_ref=dst, send_sem=s_sem, recv_sem=r_sem,
            device_id=(rep, grp, hid), device_id_type=MESH,
        )

    barrier = pltpu.get_barrier_semaphore()
    peers = [(group_of(i), h) for i in range(1, groups)] + [(g, over), (g, sib)]
    for grp, hid in peers:
        pl.semaphore_signal(barrier, inc=1, device_id=(rep, grp, hid), device_id_type=MESH)

    pairs = 2 * tokens
    named = jnp.concatenate([routes[:, 0:1], routes[:, 1:2]], axis=0)
    onehot = named == lax.broadcasted_iota(jnp.int32, (pairs, 128), 1)
    before = lax.broadcasted_iota(jnp.int32, (pairs, pairs), 0) > lax.broadcasted_iota(
        jnp.int32, (pairs, pairs), 1
    )
    earlier = nn(before.astype(F32).astype(BF16), onehot.astype(F32).astype(BF16))
    slot = jnp.sum(jnp.where(onehot, earlier, 0.0), axis=1, keepdims=True).astype(jnp.int32)
    upper = (slot >= quarter).astype(jnp.int32)
    place = upper * (gq - quarter) + named * quarter + slot
    at = (place == lax.broadcasted_iota(jnp.int32, (pairs, 2 * gq), 1)).astype(F32)
    picks[...] = at.astype(BF16)
    places[...] = at.T.astype(BF16)

    pl.semaphore_wait(barrier, len(peers))

    def cot(cols):
        wide = gout[:, cols].astype(F32)
        return jnp.concatenate(
            [(gates[:, 0:1] * wide).astype(BF16), (gates[:, 1:2] * wide).astype(BF16)], axis=0
        )

    def z_copy(k, i):
        dest = group_of(i)
        return remote(
            send.at[k, pl.ds(pl.multiple_of(dest * quarter, 16), quarter), :],
            rows[k].at[block(c, g), xcols], zs.at[k, i], zr.at[k, i], dest, h,
        )

    def x_copy(k, i):
        ref = rows[k].at[block(c, group_of(-i)), xcols]
        return remote(ref, ref, xs.at[k, i], xr.at[k, i], g, over)

    def c_copy(k, i):
        ref = rows[k].at[block(c, group_of(-i)), :]
        return remote(ref, ref, cs.at[k, i], cr.at[k, i], g, sib)

    others = range(1, groups)
    mine = places[pl.ds(pl.multiple_of(c * gq, 16), gq), :]
    send[0] = nn(mine[:, :tokens] + mine[:, tokens:], tok[:, xcols]).astype(BF16)
    for i in others:
        z_copy(0, i).start()
    send[1] = nn(mine, cot(xcols)).astype(BF16)
    for i in others:
        z_copy(1, i).start()
    for half in range(2):
        own = places[block(half, g), :]
        rows_x[block(half, g), :] = nn(own[:, :tokens] + own[:, tokens:], tok[...]).astype(BF16)
        for n in range(2):
            cols = slice(n * hc, n * hc + hc)
            rows_c[block(half, g), cols] = nn(own, cot(cols)).astype(BF16)

    def pass_over(k):
        for i in others:
            z_copy(k, i).wait_recv()
            x_copy(k, i).start()

    def pass_sib(k):
        for i in others:
            x_copy(k, i).wait_recv()
            c_copy(k, i).start()

    def arrived(k):
        for i in others:
            c_copy(k, i).wait_recv()

    pass_over(0)
    pass_sib(0)
    arrived(0)
    pass_over(1)

    def at_tile(n):
        return pl.ds(pl.multiple_of(n * tile, tile), tile)

    stores = []

    def store(src, dst):
        stores.append(pltpu.make_async_copy(src, dst, lsem.at[len(stores)]))
        stores[-1].start()

    store(rows_x, x_any)
    loads[0].wait()
    loads[1].wait()

    @pl.loop(0, ff // tile)
    def _(n):
        cols = at_tile(n)
        gate = nn(rows_x[...], wg[:, cols])
        up = nn(rows_x[...], wu[:, cols])
        sigma = jax.nn.sigmoid(gate)
        act = gate * sigma
        silu[:, cols] = act
        upslope[:, cols] = up * (sigma * (1.0 + gate * (1.0 - sigma)))
        hidden[:, cols] = (act * up).astype(BF16)

    store(hidden, hid_any)
    pass_sib(1)
    loads[2].wait()
    other_rows = pl.ds(pl.multiple_of((1 - c) * gq, 16), gq)

    @pl.loop(0, width // tile)
    def _(n):
        cols = at_tile(n)
        acc[0, :, cols] = nn(hidden[...], wd[:, cols])
        pair_send[0, :, cols] = acc[0, other_rows, cols].astype(BF16)

    def part(group):
        return pl.ds(pl.multiple_of(group * quarter, 16), quarter)

    def pair_copy(k, i):
        at_ = part(group_of(i))
        return remote(
            pair_send.at[k, at_, :], pair_recv.at[k, at_, :], c2s.at[k, i], c2r.at[k, i], g, sib
        )

    def cross_copy(k, i):
        at_ = part(group_of(i))
        return remote(
            x_send.at[k, at_, :], x_recv.at[k, at_, :], x2s.at[k, i], x2r.at[k, i], g, over
        )

    def home_copy(k, i):
        dest = group_of(i)
        return remote(
            z_send.at[k, part(dest), :], home.at[k, block(c, g), :],
            z2s.at[k, i], z2r.at[k, i], dest, h,
        )

    def twin_copy(k, i):
        ref = home.at[k, block(c, group_of(-i)), :]
        return remote(ref, ref, h2s.at[k, i], h2r.at[k, i], g, sib)

    order = list(others) + [0]

    def start_pair(k):
        for i in order:
            pair_copy(k, i).start()

    def cross(k):
        for i in order:
            pair_copy(k, i).wait_recv()
            here, there = block(c, group_of(i)), part(group_of(i))
            x_send[k, there, :] = (
                acc[k, here, ocols] + pair_recv[k, there, ocols].astype(F32)
            ).astype(BF16)
            cross_copy(k, i).start()
            acc[k, here, xcols] = acc[k, here, xcols] + pair_recv[k, there, xcols].astype(F32)

    def go_home(k):
        for i in order:
            cross_copy(k, i).wait_recv()
            here, there = block(c, group_of(i)), part(group_of(i))
            total = (acc[k, here, xcols] + x_recv[k, there, :].astype(F32)).astype(BF16)
            if i == 0:
                home[k, here, :] = total
                twin_copy(k, 0).start()
            else:
                z_send[k, there, :] = total
                home_copy(k, i).start()

    def twin(k):
        for i in others:
            home_copy(k, i).wait_recv()
            twin_copy(k, i).start()

    def out_copy(k):
        return remote(
            out_send.at[k], out_full.at[k, :, xcols], os_.at[k], or_.at[k], g, over
        )

    def combine(k):
        for i in order:
            twin_copy(k, i).wait_recv()
        for to in (1 - x, x):
            base = pl.multiple_of(to * (2 * share) + c * share, 16)
            first = picks[pl.ds(base, share), :]
            second = picks[pl.ds(base + tokens, share), :]
            if k == 0:
                w = gates[pl.ds(base, share), :]
                value = w[:, 0:1] * nn(first, home[0]) + w[:, 1:2] * nn(second, home[0])
            else:
                value = nn(first + second, home[1])
            if to is x:
                out_full[k, :, xcols] = value.astype(BF16)
            else:
                out_send[k] = value.astype(BF16)
                out_copy(k).start()

    start_pair(0)
    arrived(1)
    store(rows_c, c_any)

    @pl.loop(0, ff // tile)
    def _(n):
        cols = at_tile(n)
        back = nt(rows_c[...], wd[cols, :])
        gpg[:, cols] = (back * upslope[:, cols]).astype(BF16)
        gpu[:, cols] = (back * silu[:, cols]).astype(BF16)

    store(gpg, gpg_any)
    store(gpu, gpu_any)
    cross(0)

    @pl.loop(0, width // tile)
    def _(n):
        cols = at_tile(n)
        acc[1, :, cols] = nt(gpg[...], wg[cols, :]) + nt(gpu[...], wu[cols, :])
        pair_send[1, :, cols] = acc[1, other_rows, cols].astype(BF16)

    start_pair(1)
    go_home(0)
    cross(1)
    go_home(1)
    twin(0)
    combine(0)
    twin(1)
    combine(1)
    for k in range(2):
        out_copy(k).wait_recv()
    mixed_out[...] = out_full[0]
    gtok_out[...] = out_full[1]

    for k in range(2):
        for i in others:
            z_copy(k, i).wait_send()
            x_copy(k, i).wait_send()
            c_copy(k, i).wait_send()
            home_copy(k, i).wait_send()
        for i in order:
            pair_copy(k, i).wait_send()
            cross_copy(k, i).wait_send()
            twin_copy(k, i).wait_send()
        out_copy(k).wait_send()
    for s in stores:
        s.wait()


def fits(tokens, capacity, shares, width, ff):
    return (
        shares == 4
        and capacity % 32 == 0
        and tokens % 64 == 0
        and width % 256 == 0
        and ff % 256 == 0
    )


def local_fused(tokens, routes, gates, grad_out, w_gate, w_up, w_down):
    groups = lax.axis_size("grp")
    tok_rows, width = tokens.shape
    ff = w_gate.shape[2]
    capacity = capacity_of(tok_rows, routes.shape[1], groups)
    quarter = capacity // 2
    tile = 256
    rows = groups * capacity
    half_rows, hc = rows // 2, width // 2
    share = tok_rows // 4
    vmem = pl.BlockSpec(memory_space=pltpu.VMEM)
    hbm = pl.BlockSpec(memory_space=pl.ANY)
    dma = pltpu.SemaphoreType.DMA
    flops = 2 * rows * width * ff * 6
    rows_x, rows_c, hidden, gpg, gpu, mixed, grad_tokens = pl.pallas_call(
        functools.partial(layer_kernel, groups, quarter, tile),
        out_shape=[
            jax.ShapeDtypeStruct((rows, width), BF16),
            jax.ShapeDtypeStruct((rows, width), BF16),
            jax.ShapeDtypeStruct((rows, ff), BF16),
            jax.ShapeDtypeStruct((rows, ff), BF16),
            jax.ShapeDtypeStruct((rows, ff), BF16),
            jax.ShapeDtypeStruct((share, width), BF16),
            jax.ShapeDtypeStruct((share, width), BF16),
        ],
        in_specs=[vmem] * 4 + [hbm] * 3,
        out_specs=[hbm] * 5 + [vmem] * 2,
        scratch_shapes=[
            pltpu.VMEM((width, ff), BF16),
            pltpu.VMEM((width, ff), BF16),
            pltpu.VMEM((ff, width), BF16),
            pltpu.VMEM((rows, width), BF16),
            pltpu.VMEM((rows, width), BF16),
            pltpu.VMEM((2, half_rows, hc), BF16),
            pltpu.VMEM((rows, 2 * tok_rows), BF16),
            pltpu.VMEM((2 * tok_rows, rows), BF16),
            pltpu.VMEM((rows, ff), F32),
            pltpu.VMEM((rows, ff), F32),
            pltpu.VMEM((rows, ff), BF16),
            pltpu.VMEM((rows, ff), BF16),
            pltpu.VMEM((rows, ff), BF16),
            pltpu.VMEM((2, rows, width), F32),
            pltpu.VMEM((2, half_rows, width), BF16),
            pltpu.VMEM((2, half_rows, width), BF16),
            pltpu.VMEM((2, half_rows, hc), BF16),
            pltpu.VMEM((2, half_rows, hc), BF16),
            pltpu.VMEM((2, half_rows, hc), BF16),
            pltpu.VMEM((2, rows, hc), BF16),
            pltpu.VMEM((2, share, hc), BF16),
            pltpu.VMEM((2, share, width), BF16),
        ]
        + [dma((2, groups))] * 14
        + [dma((2,)), dma((2,)), dma((3,)), dma((5,))],
        compiler_params=pltpu.CompilerParams(
            collective_id=0, has_side_effects=True, vmem_limit_bytes=56 * 1024 * 1024
        ),
        cost_estimate=pl.CostEstimate(
            flops=flops, bytes_accessed=6 * width * ff, transcendentals=rows * ff
        ),
    )(tokens, routes, gates, grad_out, w_gate[0], w_up[0], w_down[0])
    grads = [
        lax.dot_general(a, b, (((0,), (0,)), ((), ())), preferred_element_type=F32).astype(BF16)
        for a, b in ((rows_x, gpg), (rows_x, gpu), (hidden, rows_c))
    ]
    return (mixed, grad_tokens, grads[0][None], grads[1][None], grads[2][None])


def capacity_of(tok_rows, top_count, groups):
    return max(3 * tok_rows // 8, top_count * tok_rows // groups)


def slot_numbers(route_blocks, expert_count):
    onehot = (route_blocks[..., None] == jnp.arange(expert_count, dtype=jnp.int32)).astype(
        jnp.int32
    )
    earlier = jnp.cumsum(onehot, axis=-2) - onehot
    return jnp.sum(earlier * onehot, axis=-1)


def forward_rows(rows_x, weight_gate, weight_up, weight_down):
    gate_pre = jnp.dot(rows_x, weight_gate, preferred_element_type=jnp.float32)
    up_pre = jnp.dot(rows_x, weight_up, preferred_element_type=jnp.float32)
    sigma_gate = jax.nn.sigmoid(gate_pre)
    silu_gate = gate_pre * sigma_gate
    hidden = (silu_gate * up_pre).astype(jnp.bfloat16)
    expert_out = jnp.dot(hidden, weight_down, preferred_element_type=jnp.float32)
    return (gate_pre, up_pre, sigma_gate, silu_gate, hidden, expert_out)


def backward_rows(rows_x, rows_c, weight_gate, weight_up, weight_down, saved):
    gate_pre, up_pre, sigma_gate, silu_gate, hidden, expert_out = saved
    grad_hidden = jnp.dot(rows_c, weight_down.T, preferred_element_type=jnp.float32)
    slope = sigma_gate * (1.0 + gate_pre * (1.0 - sigma_gate))
    grad_pre_gate = (grad_hidden * up_pre * slope).astype(jnp.bfloat16)
    grad_pre_up = (grad_hidden * silu_gate).astype(jnp.bfloat16)
    grad_rows = jnp.dot(grad_pre_gate, weight_gate.T, preferred_element_type=jnp.float32)
    grad_rows = grad_rows + jnp.dot(grad_pre_up, weight_up.T, preferred_element_type=jnp.float32)
    grad_wgate = jnp.dot(rows_x.T, grad_pre_gate, preferred_element_type=jnp.float32).astype(
        jnp.bfloat16
    )
    grad_wup = jnp.dot(rows_x.T, grad_pre_up, preferred_element_type=jnp.float32).astype(
        jnp.bfloat16
    )
    grad_wdown = jnp.dot(hidden.T, rows_c, preferred_element_type=jnp.float32).astype(jnp.bfloat16)
    return (grad_rows, grad_wgate, grad_wup, grad_wdown)


def combine_pairs(whole, weights, row_ids):
    members, groups, capacity, width = whole.shape
    tok_count, top_count = row_ids.shape
    flat = whole.reshape(members, groups * capacity, width)
    picked = jnp.take(flat, row_ids.reshape(-1), axis=1).reshape(
        members, tok_count, top_count, width
    )
    return jnp.sum(weights[..., None] * picked, axis=2)


def send_back(stacked, weights, target_row):
    shares = lax.axis_size("hid")
    share = lax.axis_index("hid")
    tok_rows, top_count = target_row.shape
    summed = lax.psum_scatter(stacked, "hid", scatter_dimension=2, tiled=True)
    moved = lax.all_to_all(summed, "grp", split_axis=1, concat_axis=1, tiled=True)
    whole = lax.all_gather(moved, "hid", axis=2, tiled=True)
    own_count = tok_rows // shares
    own_rows = lax.dynamic_slice_in_dim(target_row, share * own_count, own_count, 0)
    own_weights = lax.dynamic_slice_in_dim(weights, share * own_count, own_count, 1)
    return combine_pairs(whole, own_weights, own_rows)


def local_plain(tokens, routes, gates, grad_out, w_gate, w_up, w_down):
    groups = lax.axis_size("grp")
    shares = lax.axis_size("hid")
    share = lax.axis_index("hid")
    tok_rows, width = tokens.shape
    top_count = routes.shape[1]
    capacity = max(3 * tok_rows // 8, top_count * tok_rows // groups)
    part_slots = capacity // shares
    pairs = tok_rows * top_count
    flat_routes = routes.T.reshape(pairs)
    slot_index = slot_numbers(flat_routes[None, :], groups)[0]
    target_row = flat_routes * capacity + slot_index
    wanted = (
        jnp.arange(groups, dtype=jnp.int32)[:, None] * capacity
        + share * part_slots
        + jnp.arange(part_slots, dtype=jnp.int32)[None, :]
    ).reshape(-1)
    placer = (wanted[:, None] == target_row[None, :]).astype(jnp.bfloat16)
    tok_pairs = jnp.tile(tokens, (top_count, 1))
    cot_pairs = (
        gates.T.reshape(pairs, 1) * jnp.tile(grad_out, (top_count, 1)).astype(jnp.float32)
    ).astype(jnp.bfloat16)
    send_x = (
        jnp.dot(placer, tok_pairs, preferred_element_type=jnp.float32)
        .astype(jnp.bfloat16)
        .reshape(groups, part_slots, width)
    )
    send_c = (
        jnp.dot(placer, cot_pairs, preferred_element_type=jnp.float32)
        .astype(jnp.bfloat16)
        .reshape(groups, part_slots, width)
    )
    arrived = (
        lax.all_to_all(send_x, "grp", split_axis=0, concat_axis=0, tiled=True),
        lax.all_to_all(send_c, "grp", split_axis=0, concat_axis=0, tiled=True),
    )
    block_x, block_c = (
        lax.all_gather(arrived[0], "hid", axis=1, tiled=True),
        lax.all_gather(arrived[1], "hid", axis=1, tiled=True),
    )
    block_shape = block_x.shape
    rows_x = block_x.reshape(-1, width)
    rows_c = block_c.reshape(-1, width)
    weight_gate = w_gate[0]
    weight_up = w_up[0]
    weight_down = w_down[0]
    row_table = target_row.reshape(top_count, tok_rows).T
    plain = jnp.ones_like(gates)
    saved = forward_rows(rows_x, weight_gate, weight_up, weight_down)
    out_terms = saved[5].reshape(block_shape)
    grad_rows, grad_wgate, grad_wup, grad_wdown = backward_rows(
        rows_x, rows_c, weight_gate, weight_up, weight_down, saved
    )
    home_both = send_back(
        jnp.stack([out_terms, grad_rows.reshape(block_shape)]), jnp.stack([gates, plain]), row_table
    )
    home_out = home_both[0]
    home_grad = home_both[1]
    mixed = home_out.astype(jnp.bfloat16)
    grad_tokens = home_grad.astype(jnp.bfloat16)
    return (mixed, grad_tokens, grad_wgate[None], grad_wup[None], grad_wdown[None])


def local(tokens, routes, gates, grad_out, w_gate, w_up, w_down):
    capacity = capacity_of(tokens.shape[0], routes.shape[1], lax.axis_size("grp"))
    args = (tokens, routes, gates, grad_out, w_gate, w_up, w_down)
    shares = lax.axis_size("hid")
    if fits(tokens.shape[0], capacity, shares, tokens.shape[1], w_gate.shape[2]):
        return local_fused(*args)
    return local_plain(*args)


def solution(mesh):
    in_specs = (
        P(("rep", "grp"), None),
        P(("rep", "grp"), None),
        P(("rep", "grp"), None),
        P(("rep", "grp"), None),
        P("grp", None, "hid"),
        P("grp", None, "hid"),
        P("grp", "hid", None),
    )
    out_specs = (
        P(("rep", "grp", "hid"), None),
        P(("rep", "grp", "hid"), None),
        P(("rep", "grp"), None, "hid"),
        P(("rep", "grp"), None, "hid"),
        P(("rep", "grp"), "hid", None),
    )
    return jax.shard_map(local, mesh=mesh, in_specs=in_specs, out_specs=out_specs, check_vma=False)
```

```python
import functools

import jax
import jax.numpy as jnp
from jax import lax
from jax.experimental import pallas as pl
from jax.experimental.pallas import tpu as pltpu
from jax.sharding import PartitionSpec as P

MESH = pl.DeviceIdType.MESH
F32 = jnp.float32
BF16 = jnp.bfloat16


UNROLL = 8


def nn(a, b):
    return jnp.dot(a, b, preferred_element_type=F32)


def nt(a, b):
    return lax.dot_general(a, b, (((1,), (1,)), ((), ())), preferred_element_type=F32)


def column(row):
    size = row.shape[1]
    square = (size, size)
    diagonal = lax.broadcasted_iota(jnp.int32, square, 0) == lax.broadcasted_iota(
        jnp.int32, square, 1
    )
    return jnp.sum(jnp.where(diagonal, row, 0.0), axis=1, keepdims=True)


def layer_kernel(
    groups, quarter, tile,
    tok, routes, gates_row, gout, wg_any, wu_any, wd_any,
    xt_any, c_any, hidt_any, gpg_any, gpu_any, mixed_out, gtok_out,
    wg, wu, wd, rows_x, rows_c, send, places, picks, silu, upslope, hidden, gpg, gpu,
    rows_xt, hidden_t, gates, acc, pair_send, pair_recv, x_send, x_recv, z_send, home, out_send, out_full,
    zs, zr, xs, xr, cs, cr, c2s, c2r, x2s, x2r, z2s, z2r, h2s, h2r, os_, or_, wsem, lsem,
):
    rep = lax.axis_index("rep")
    g = lax.axis_index("grp")
    h = lax.axis_index("hid")
    x = h // 2
    c = lax.rem(h, 2)
    over = (1 - x) * 2 + c
    sib = x * 2 + 1 - c
    tokens, width = tok.shape
    hc = width // 2
    gq = groups * quarter
    ff = hidden.shape[1]
    share = tokens // 4
    xcols = pl.ds(pl.multiple_of(x * hc, 128), hc)
    ocols = pl.ds(pl.multiple_of((1 - x) * hc, 128), hc)
    rows = (rows_x, rows_c)

    loads = [
        pltpu.make_async_copy(a, b, wsem.at[i])
        for i, (a, b) in enumerate(((wg_any, wg), (wu_any, wu), (wd_any, wd)))
    ]
    for load in loads:
        load.start()

    def group_of(shift):
        return lax.rem(g + shift + groups, groups)

    def block(half, group):
        return pl.ds(pl.multiple_of(half * gq + group * quarter, 16), quarter)

    def remote(src, dst, s_sem, r_sem, grp, hid):
        return pltpu.make_async_remote_copy(
            src_ref=src, dst_ref=dst, send_sem=s_sem, recv_sem=r_sem,
            device_id=(rep, grp, hid), device_id_type=MESH,
        )

    barrier = pltpu.get_barrier_semaphore()
    peers = [(group_of(i), h) for i in range(1, groups)] + [(g, over), (g, sib)]
    for grp, hid in peers:
        pl.semaphore_signal(barrier, inc=1, device_id=(rep, grp, hid), device_id_type=MESH)

    pairs = 2 * tokens
    wide_routes = routes[...].astype(F32)
    named = jnp.concatenate(
        [column(wide_routes[0:1, :]), column(wide_routes[1:2, :])], axis=0
    ).astype(jnp.int32)
    for n in range(2):
        gates[:, n : n + 1] = column(gates_row[n : n + 1, :])
    onehot = named == lax.broadcasted_iota(jnp.int32, (pairs, 128), 1)
    before = lax.broadcasted_iota(jnp.int32, (pairs, pairs), 0) > lax.broadcasted_iota(
        jnp.int32, (pairs, pairs), 1
    )
    earlier = nn(before.astype(F32).astype(BF16), onehot.astype(F32).astype(BF16))
    slot = jnp.sum(jnp.where(onehot, earlier, 0.0), axis=1, keepdims=True).astype(jnp.int32)
    upper = (slot >= quarter).astype(jnp.int32)
    place = upper * (gq - quarter) + named * quarter + slot
    at = (place == lax.broadcasted_iota(jnp.int32, (pairs, 2 * gq), 1)).astype(F32)
    picks[...] = at.astype(BF16)
    places[...] = at.T.astype(BF16)

    pl.semaphore_wait(barrier, len(peers))

    def cot(cols):
        wide = gout[:, cols].astype(F32)
        return jnp.concatenate(
            [(gates[:, 0:1] * wide).astype(BF16), (gates[:, 1:2] * wide).astype(BF16)], axis=0
        )

    def z_copy(k, i):
        dest = group_of(i)
        return remote(
            send.at[k, pl.ds(pl.multiple_of(dest * quarter, 16), quarter), :],
            rows[k].at[block(c, g), xcols], zs.at[k, i], zr.at[k, i], dest, h,
        )

    def x_copy(k, i):
        ref = rows[k].at[block(c, group_of(-i)), xcols]
        return remote(ref, ref, xs.at[k, i], xr.at[k, i], g, over)

    def c_copy(k, i):
        ref = rows[k].at[block(c, group_of(-i)), :]
        return remote(ref, ref, cs.at[k, i], cr.at[k, i], g, sib)

    others = range(1, groups)
    mine = places[pl.ds(pl.multiple_of(c * gq, 16), gq), :]
    send[0] = nn(mine[:, :tokens] + mine[:, tokens:], tok[:, xcols]).astype(BF16)
    for i in others:
        z_copy(0, i).start()
    send[1] = nn(mine, cot(xcols)).astype(BF16)
    for half in range(2):
        own = places[block(half, g), :]
        rows_x[block(half, g), :] = nn(own[:, :tokens] + own[:, tokens:], tok[...]).astype(BF16)
        for n in range(2):
            cols = slice(n * hc, n * hc + hc)
            rows_c[block(half, g), cols] = nn(own, cot(cols)).astype(BF16)

    def pass_over(k):
        for i in others:
            z_copy(k, i).wait_recv()
            x_copy(k, i).start()

    def pass_sib(k):
        for i in others:
            x_copy(k, i).wait_recv()
            c_copy(k, i).start()

    def arrived(k):
        for i in others:
            c_copy(k, i).wait_recv()

    pass_over(0)
    for i in others:
        z_copy(1, i).start()
    pass_sib(0)
    arrived(0)
    pass_over(1)

    def at_tile(n):
        return pl.ds(pl.multiple_of(n * tile, tile), tile)

    stores = []

    def store(src, dst):
        stores.append(pltpu.make_async_copy(src, dst, lsem.at[len(stores)]))
        stores[-1].start()

    loads[0].wait()
    loads[1].wait()

    @pl.loop(0, ff // tile, unroll=UNROLL)
    def _(n):
        cols = at_tile(n)
        gate = nn(rows_x[...], wg[:, cols])
        up = nn(rows_x[...], wu[:, cols])
        sigma = jax.nn.sigmoid(gate)
        act = gate * sigma
        silu[:, cols] = act
        upslope[:, cols] = up * (sigma * (1.0 + gate * (1.0 - sigma)))
        hidden[:, cols] = (act * up).astype(BF16)

    pass_sib(1)
    loads[2].wait()
    other_rows = pl.ds(pl.multiple_of((1 - c) * gq, 16), gq)

    @pl.loop(0, width // tile, unroll=UNROLL)
    def _(n):
        cols = at_tile(n)
        acc[0, :, cols] = nn(hidden[...], wd[:, cols])
        pair_send[0, :, cols] = acc[0, other_rows, cols].astype(BF16)

    def part(group):
        return pl.ds(pl.multiple_of(group * quarter, 16), quarter)

    def pair_copy(k, i, n):
        at_, cols = part(group_of(i)), (ocols, xcols)[n]
        j = i + n * groups
        return remote(
            pair_send.at[k, at_, cols], pair_recv.at[k, at_, cols],
            c2s.at[k, j], c2r.at[k, j], g, sib,
        )

    def cross_copy(k, i):
        at_ = part(group_of(i))
        return remote(
            x_send.at[k, at_, :], x_recv.at[k, at_, :], x2s.at[k, i], x2r.at[k, i], g, over
        )

    def home_copy(k, i):
        dest = group_of(i)
        return remote(
            z_send.at[k, part(dest), :], home.at[k, block(c, g), :],
            z2s.at[k, i], z2r.at[k, i], dest, h,
        )

    def twin_copy(k, i):
        ref = home.at[k, block(c, group_of(-i)), :]
        return remote(ref, ref, h2s.at[k, i], h2r.at[k, i], g, sib)

    order = list(others) + [0]

    def start_pair(k, n):
        for i in order:
            pair_copy(k, i, n).start()

    def cross(k):
        for i in order:
            pair_copy(k, i, 0).wait_recv()
            here, there = block(c, group_of(i)), part(group_of(i))
            x_send[k, there, :] = (
                acc[k, here, ocols] + pair_recv[k, there, ocols].astype(F32)
            ).astype(BF16)
            cross_copy(k, i).start()

    def go_home(k):
        for i in order:
            pair_copy(k, i, 1).wait_recv()
            cross_copy(k, i).wait_recv()
            here, there = block(c, group_of(i)), part(group_of(i))
            total = (
                (acc[k, here, xcols] + pair_recv[k, there, xcols].astype(F32))
                + x_recv[k, there, :].astype(F32)
            ).astype(BF16)
            if i == 0:
                home[k, here, :] = total
                twin_copy(k, 0).start()
            else:
                z_send[k, there, :] = total
                home_copy(k, i).start()

    def twin(k):
        for i in others:
            home_copy(k, i).wait_recv()
            twin_copy(k, i).start()

    def out_copy(k):
        return remote(
            out_send.at[k], out_full.at[k, :, xcols], os_.at[k], or_.at[k], g, over
        )

    def combine(k):
        for i in order:
            twin_copy(k, i).wait_recv()
        for to in (1 - x, x):
            base = pl.multiple_of(to * (2 * share) + c * share, 16)
            first = picks[pl.ds(base, share), :]
            second = picks[pl.ds(base + tokens, share), :]
            if k == 0:
                w = gates[pl.ds(base, share), :]
                value = w[:, 0:1] * nn(first, home[0]) + w[:, 1:2] * nn(second, home[0])
            else:
                value = nn(first + second, home[1])
            if to is x:
                out_full[k, :, xcols] = value.astype(BF16)
            else:
                out_send[k] = value.astype(BF16)
                out_copy(k).start()

    start_pair(0, 0)
    start_pair(0, 1)
    arrived(1)
    store(rows_c, c_any)

    def back_tiles(first, last):
        @pl.loop(first, last, unroll=UNROLL)
        def _(n):
            cols = at_tile(n)
            back = nt(rows_c[...], wd[cols, :])
            gpg[:, cols] = (back * upslope[:, cols]).astype(BF16)
            gpu[:, cols] = (back * silu[:, cols]).astype(BF16)

    tiles = ff // tile
    back_tiles(0, tiles // 2)
    cross(0)
    back_tiles(tiles // 2, tiles)
    store(gpg, gpg_any)
    store(gpu, gpu_any)

    def grad_cols(cols):
        acc[1, :, cols] = nt(gpg[...], wg[cols, :]) + nt(gpu[...], wu[cols, :])
        pair_send[1, :, cols] = acc[1, other_rows, cols].astype(BF16)

    for n, side in enumerate((1 - x, x)):

        @pl.loop(0, hc // tile, unroll=UNROLL)
        def _(j):
            grad_cols(pl.ds(pl.multiple_of(side * hc + j * tile, 128), tile))

        rest = hc % tile
        if rest:
            grad_cols(pl.ds(pl.multiple_of(side * hc + hc - rest, 128), rest))
        start_pair(1, n)

    cross(1)
    go_home(0)

    @pl.loop(0, width // tile)
    def _(n):
        rows_xt[at_tile(n), :] = rows_x[:, at_tile(n)].T

    store(rows_xt, xt_any)
    go_home(1)

    @pl.loop(0, tiles)
    def _(n):
        hidden_t[at_tile(n), :] = hidden[:, at_tile(n)].T

    store(hidden_t, hidt_any)
    twin(0)
    combine(0)
    twin(1)
    combine(1)
    for k in range(2):
        out_copy(k).wait_recv()
    mixed_out[...] = out_full[0]
    gtok_out[...] = out_full[1]

    for k in range(2):
        for i in others:
            z_copy(k, i).wait_send()
            x_copy(k, i).wait_send()
            c_copy(k, i).wait_send()
            home_copy(k, i).wait_send()
        for i in order:
            pair_copy(k, i, 0).wait_send()
            pair_copy(k, i, 1).wait_send()
            cross_copy(k, i).wait_send()
            twin_copy(k, i).wait_send()
        out_copy(k).wait_send()
    for s in stores:
        s.wait()


def weights_kernel(
    rows_xt, hidden_t, gpg, gpu, rows_c, mixed, gtok,
    mixed_out, gtok_out, grad_gate, grad_up, grad_down,
):
    @pl.when(pl.program_id(0) == 0)
    def _():
        mixed_out[...] = mixed[...]
        gtok_out[...] = gtok[...]

    grad_gate[...] = nn(rows_xt[...], gpg[...]).astype(BF16)
    grad_up[...] = nn(rows_xt[...], gpu[...]).astype(BF16)
    grad_down[...] = nn(hidden_t[...], rows_c[...]).astype(BF16)


def fits(tokens, capacity, shares, width, ff):
    return (
        shares == 4
        and capacity % 32 == 0
        and tokens % 64 == 0
        and width % 256 == 0
        and ff % 256 == 0
    )


def local_fused(tokens, routes, gates, grad_out, w_gate, w_up, w_down):
    groups = lax.axis_size("grp")
    tok_rows, width = tokens.shape
    ff = w_gate.shape[2]
    capacity = capacity_of(tok_rows, routes.shape[1], groups)
    quarter = capacity // 2
    tile = 256
    rows = groups * capacity
    half_rows, hc = rows // 2, width // 2
    share = tok_rows // 4
    vmem = pl.BlockSpec(memory_space=pltpu.VMEM)
    hbm = pl.BlockSpec(memory_space=pl.ANY)
    dma = pltpu.SemaphoreType.DMA
    flops = 2 * rows * width * ff * 6
    rows_xt, rows_c, hidden_t, gpg, gpu, mixed, grad_tokens = pl.pallas_call(
        functools.partial(layer_kernel, groups, quarter, tile),
        out_shape=[
            jax.ShapeDtypeStruct((width, rows), BF16),
            jax.ShapeDtypeStruct((rows, width), BF16),
            jax.ShapeDtypeStruct((ff, rows), BF16),
            jax.ShapeDtypeStruct((rows, ff), BF16),
            jax.ShapeDtypeStruct((rows, ff), BF16),
            jax.ShapeDtypeStruct((share, width), BF16),
            jax.ShapeDtypeStruct((share, width), BF16),
        ],
        in_specs=[vmem] * 4 + [hbm] * 3,
        out_specs=[hbm] * 5 + [vmem] * 2,
        scratch_shapes=[
            pltpu.VMEM((width, ff), BF16),
            pltpu.VMEM((width, ff), BF16),
            pltpu.VMEM((ff, width), BF16),
            pltpu.VMEM((rows, width), BF16),
            pltpu.VMEM((rows, width), BF16),
            pltpu.VMEM((2, half_rows, hc), BF16),
            pltpu.VMEM((rows, 2 * tok_rows), BF16),
            pltpu.VMEM((2 * tok_rows, rows), BF16),
            pltpu.VMEM((rows, ff), F32),
            pltpu.VMEM((rows, ff), F32),
            pltpu.VMEM((rows, ff), BF16),
            pltpu.VMEM((rows, ff), BF16),
            pltpu.VMEM((rows, ff), BF16),
            pltpu.VMEM((width, rows), BF16),
            pltpu.VMEM((ff, rows), BF16),
            pltpu.VMEM((tok_rows, 2), F32),
            pltpu.VMEM((2, rows, width), F32),
            pltpu.VMEM((2, half_rows, width), BF16),
            pltpu.VMEM((2, half_rows, width), BF16),
            pltpu.VMEM((2, half_rows, hc), BF16),
            pltpu.VMEM((2, half_rows, hc), BF16),
            pltpu.VMEM((2, half_rows, hc), BF16),
            pltpu.VMEM((2, rows, hc), BF16),
            pltpu.VMEM((2, share, hc), BF16),
            pltpu.VMEM((2, share, width), BF16),
        ]
        + [dma((2, groups))] * 6
        + [dma((2, 2 * groups))] * 2
        + [dma((2, groups))] * 6
        + [dma((2,)), dma((2,)), dma((3,)), dma((5,))],
        compiler_params=pltpu.CompilerParams(
            collective_id=0, has_side_effects=True, vmem_limit_bytes=56 * 1024 * 1024
        ),
        cost_estimate=pl.CostEstimate(
            flops=flops, bytes_accessed=6 * width * ff, transcendentals=rows * ff
        ),
    )(tokens, routes.T, gates.T, grad_out, w_gate[0], w_up[0], w_down[0])
    steps = 6 if ff % 768 == 0 and width % 768 == 0 else 2
    wide, narrow = width // steps, ff // steps
    whole = lambda shape: pl.BlockSpec(shape, lambda n: (0, 0))
    side = lambda shape: pl.BlockSpec(shape, lambda n: (0, n))
    mixed, grad_tokens, grad_gate, grad_up, grad_down = pl.pallas_call(
        weights_kernel,
        grid=(steps,),
        out_shape=[
            jax.ShapeDtypeStruct((share, width), BF16),
            jax.ShapeDtypeStruct((share, width), BF16),
            jax.ShapeDtypeStruct((width, ff), BF16),
            jax.ShapeDtypeStruct((width, ff), BF16),
            jax.ShapeDtypeStruct((ff, width), BF16),
        ],
        in_specs=[
            whole((width, rows)),
            whole((ff, rows)),
            side((rows, narrow)),
            side((rows, narrow)),
            side((rows, wide)),
            whole((share, width)),
            whole((share, width)),
        ],
        out_specs=[
            whole((share, width)),
            whole((share, width)),
            side((width, narrow)),
            side((width, narrow)),
            side((ff, wide)),
        ],
        compiler_params=pltpu.CompilerParams(vmem_limit_bytes=60 * 1024 * 1024),
        cost_estimate=pl.CostEstimate(
            flops=flops // 2, bytes_accessed=6 * width * ff, transcendentals=0
        ),
    )(rows_xt, hidden_t, gpg, gpu, rows_c, mixed, grad_tokens)
    return (mixed, grad_tokens, grad_gate[None], grad_up[None], grad_down[None])


def capacity_of(tok_rows, top_count, groups):
    return max(3 * tok_rows // 8, top_count * tok_rows // groups)


def slot_numbers(route_blocks, expert_count):
    onehot = (route_blocks[..., None] == jnp.arange(expert_count, dtype=jnp.int32)).astype(
        jnp.int32
    )
    earlier = jnp.cumsum(onehot, axis=-2) - onehot
    return jnp.sum(earlier * onehot, axis=-1)


def forward_rows(rows_x, weight_gate, weight_up, weight_down):
    gate_pre = jnp.dot(rows_x, weight_gate, preferred_element_type=jnp.float32)
    up_pre = jnp.dot(rows_x, weight_up, preferred_element_type=jnp.float32)
    sigma_gate = jax.nn.sigmoid(gate_pre)
    silu_gate = gate_pre * sigma_gate
    hidden = (silu_gate * up_pre).astype(jnp.bfloat16)
    expert_out = jnp.dot(hidden, weight_down, preferred_element_type=jnp.float32)
    return (gate_pre, up_pre, sigma_gate, silu_gate, hidden, expert_out)


def backward_rows(rows_x, rows_c, weight_gate, weight_up, weight_down, saved):
    gate_pre, up_pre, sigma_gate, silu_gate, hidden, expert_out = saved
    grad_hidden = jnp.dot(rows_c, weight_down.T, preferred_element_type=jnp.float32)
    slope = sigma_gate * (1.0 + gate_pre * (1.0 - sigma_gate))
    grad_pre_gate = (grad_hidden * up_pre * slope).astype(jnp.bfloat16)
    grad_pre_up = (grad_hidden * silu_gate).astype(jnp.bfloat16)
    grad_rows = jnp.dot(grad_pre_gate, weight_gate.T, preferred_element_type=jnp.float32)
    grad_rows = grad_rows + jnp.dot(grad_pre_up, weight_up.T, preferred_element_type=jnp.float32)
    grad_wgate = jnp.dot(rows_x.T, grad_pre_gate, preferred_element_type=jnp.float32).astype(
        jnp.bfloat16
    )
    grad_wup = jnp.dot(rows_x.T, grad_pre_up, preferred_element_type=jnp.float32).astype(
        jnp.bfloat16
    )
    grad_wdown = jnp.dot(hidden.T, rows_c, preferred_element_type=jnp.float32).astype(jnp.bfloat16)
    return (grad_rows, grad_wgate, grad_wup, grad_wdown)


def combine_pairs(whole, weights, row_ids):
    members, groups, capacity, width = whole.shape
    tok_count, top_count = row_ids.shape
    flat = whole.reshape(members, groups * capacity, width)
    picked = jnp.take(flat, row_ids.reshape(-1), axis=1).reshape(
        members, tok_count, top_count, width
    )
    return jnp.sum(weights[..., None] * picked, axis=2)


def send_back(stacked, weights, target_row):
    shares = lax.axis_size("hid")
    share = lax.axis_index("hid")
    tok_rows, top_count = target_row.shape
    summed = lax.psum_scatter(stacked, "hid", scatter_dimension=2, tiled=True)
    moved = lax.all_to_all(summed, "grp", split_axis=1, concat_axis=1, tiled=True)
    whole = lax.all_gather(moved, "hid", axis=2, tiled=True)
    own_count = tok_rows // shares
    own_rows = lax.dynamic_slice_in_dim(target_row, share * own_count, own_count, 0)
    own_weights = lax.dynamic_slice_in_dim(weights, share * own_count, own_count, 1)
    return combine_pairs(whole, own_weights, own_rows)


def local_plain(tokens, routes, gates, grad_out, w_gate, w_up, w_down):
    groups = lax.axis_size("grp")
    shares = lax.axis_size("hid")
    share = lax.axis_index("hid")
    tok_rows, width = tokens.shape
    top_count = routes.shape[1]
    capacity = max(3 * tok_rows // 8, top_count * tok_rows // groups)
    part_slots = capacity // shares
    pairs = tok_rows * top_count
    flat_routes = routes.T.reshape(pairs)
    slot_index = slot_numbers(flat_routes[None, :], groups)[0]
    target_row = flat_routes * capacity + slot_index
    wanted = (
        jnp.arange(groups, dtype=jnp.int32)[:, None] * capacity
        + share * part_slots
        + jnp.arange(part_slots, dtype=jnp.int32)[None, :]
    ).reshape(-1)
    placer = (wanted[:, None] == target_row[None, :]).astype(jnp.bfloat16)
    tok_pairs = jnp.tile(tokens, (top_count, 1))
    cot_pairs = (
        gates.T.reshape(pairs, 1) * jnp.tile(grad_out, (top_count, 1)).astype(jnp.float32)
    ).astype(jnp.bfloat16)
    send_x = (
        jnp.dot(placer, tok_pairs, preferred_element_type=jnp.float32)
        .astype(jnp.bfloat16)
        .reshape(groups, part_slots, width)
    )
    send_c = (
        jnp.dot(placer, cot_pairs, preferred_element_type=jnp.float32)
        .astype(jnp.bfloat16)
        .reshape(groups, part_slots, width)
    )
    arrived = (
        lax.all_to_all(send_x, "grp", split_axis=0, concat_axis=0, tiled=True),
        lax.all_to_all(send_c, "grp", split_axis=0, concat_axis=0, tiled=True),
    )
    block_x, block_c = (
        lax.all_gather(arrived[0], "hid", axis=1, tiled=True),
        lax.all_gather(arrived[1], "hid", axis=1, tiled=True),
    )
    block_shape = block_x.shape
    rows_x = block_x.reshape(-1, width)
    rows_c = block_c.reshape(-1, width)
    weight_gate = w_gate[0]
    weight_up = w_up[0]
    weight_down = w_down[0]
    row_table = target_row.reshape(top_count, tok_rows).T
    plain = jnp.ones_like(gates)
    saved = forward_rows(rows_x, weight_gate, weight_up, weight_down)
    out_terms = saved[5].reshape(block_shape)
    grad_rows, grad_wgate, grad_wup, grad_wdown = backward_rows(
        rows_x, rows_c, weight_gate, weight_up, weight_down, saved
    )
    home_both = send_back(
        jnp.stack([out_terms, grad_rows.reshape(block_shape)]), jnp.stack([gates, plain]), row_table
    )
    home_out = home_both[0]
    home_grad = home_both[1]
    mixed = home_out.astype(jnp.bfloat16)
    grad_tokens = home_grad.astype(jnp.bfloat16)
    return (mixed, grad_tokens, grad_wgate[None], grad_wup[None], grad_wdown[None])


def local(tokens, routes, gates, grad_out, w_gate, w_up, w_down):
    capacity = capacity_of(tokens.shape[0], routes.shape[1], lax.axis_size("grp"))
    args = (tokens, routes, gates, grad_out, w_gate, w_up, w_down)
    shares = lax.axis_size("hid")
    if fits(tokens.shape[0], capacity, shares, tokens.shape[1], w_gate.shape[2]):
        return local_fused(*args)
    return local_plain(*args)


def solution(mesh):
    in_specs = (
        P(("rep", "grp"), None),
        P(("rep", "grp"), None),
        P(("rep", "grp"), None),
        P(("rep", "grp"), None),
        P("grp", None, "hid"),
        P("grp", None, "hid"),
        P("grp", "hid", None),
    )
    out_specs = (
        P(("rep", "grp", "hid"), None),
        P(("rep", "grp", "hid"), None),
        P(("rep", "grp"), None, "hid"),
        P(("rep", "grp"), None, "hid"),
        P(("rep", "grp"), "hid", None),
    )
    return jax.shard_map(local, mesh=mesh, in_specs=in_specs, out_specs=out_specs, check_vma=False)
```

```python
import functools

import jax
import jax.numpy as jnp
from jax import lax
from jax.experimental import pallas as pl
from jax.experimental.pallas import tpu as pltpu
from jax.sharding import PartitionSpec as P

MESH = pl.DeviceIdType.MESH
F32 = jnp.float32
BF16 = jnp.bfloat16


UNROLL = 8


def nn(a, b):
    return jnp.dot(a, b, preferred_element_type=F32)


def nt(a, b):
    return lax.dot_general(a, b, (((1,), (1,)), ((), ())), preferred_element_type=F32)


def column(row):
    size = row.shape[1]
    square = (size, size)
    diagonal = lax.broadcasted_iota(jnp.int32, square, 0) == lax.broadcasted_iota(
        jnp.int32, square, 1
    )
    return jnp.sum(jnp.where(diagonal, row, 0.0), axis=1, keepdims=True)


def layer_kernel(
    groups, quarter, tile,
    tok, routes, gates_row, gout, wg_any, wu_any, wd_any,
    xt_any, c_any, hidt_any, gpg_any, gpu_any, mixed_out, gtok_out,
    wg, wu, wd, rows_x, rows_c, send, places, picks, silu, upslope, hidden, gpg, gpu,
    rows_xt, hidden_t, gates, acc, pair_send, pair_recv, x_send, x_recv, z_send, home, out_send, out_full,
    zs, zr, xs, xr, cs, cr, c2s, c2r, x2s, x2r, z2s, z2r, h2s, h2r, os_, or_, wsem, lsem,
):
    rep = lax.axis_index("rep")
    g = lax.axis_index("grp")
    h = lax.axis_index("hid")
    x = h // 2
    c = lax.rem(h, 2)
    over = (1 - x) * 2 + c
    sib = x * 2 + 1 - c
    tokens, width = tok.shape
    hc = width // 2
    gq = groups * quarter
    ff = hidden.shape[1]
    share = tokens // 4
    xcols = pl.ds(pl.multiple_of(x * hc, 128), hc)
    ocols = pl.ds(pl.multiple_of((1 - x) * hc, 128), hc)
    rows = (rows_x, rows_c)

    loads = [
        pltpu.make_async_copy(a, b, wsem.at[i])
        for i, (a, b) in enumerate(((wg_any, wg), (wu_any, wu), (wd_any, wd)))
    ]
    for load in loads:
        load.start()

    def group_of(shift):
        return lax.rem(g + shift + groups, groups)

    def block(half, group):
        return pl.ds(pl.multiple_of(half * gq + group * quarter, 16), quarter)

    def remote(src, dst, s_sem, r_sem, grp, hid):
        return pltpu.make_async_remote_copy(
            src_ref=src, dst_ref=dst, send_sem=s_sem, recv_sem=r_sem,
            device_id=(rep, grp, hid), device_id_type=MESH,
        )

    barrier = pltpu.get_barrier_semaphore()
    peers = [(group_of(i), h) for i in range(1, groups)] + [(g, over), (g, sib)]
    for grp, hid in peers:
        pl.semaphore_signal(barrier, inc=1, device_id=(rep, grp, hid), device_id_type=MESH)

    pairs = 2 * tokens
    wide_routes = routes[...].astype(F32)
    named = jnp.concatenate(
        [column(wide_routes[0:1, :]), column(wide_routes[1:2, :])], axis=0
    ).astype(jnp.int32)
    for n in range(2):
        gates[:, n : n + 1] = column(gates_row[n : n + 1, :])
    onehot = named == lax.broadcasted_iota(jnp.int32, (pairs, 128), 1)
    before = lax.broadcasted_iota(jnp.int32, (pairs, pairs), 0) > lax.broadcasted_iota(
        jnp.int32, (pairs, pairs), 1
    )
    earlier = nn(before.astype(F32).astype(BF16), onehot.astype(F32).astype(BF16))
    slot = jnp.sum(jnp.where(onehot, earlier, 0.0), axis=1, keepdims=True).astype(jnp.int32)
    upper = (slot >= quarter).astype(jnp.int32)
    place = upper * (gq - quarter) + named * quarter + slot
    at = (place == lax.broadcasted_iota(jnp.int32, (pairs, 2 * gq), 1)).astype(F32)
    picks[...] = at.astype(BF16)
    places[...] = at.T.astype(BF16)

    pl.semaphore_wait(barrier, len(peers))

    def cot(cols):
        wide = gout[:, cols].astype(F32)
        return jnp.concatenate(
            [(gates[:, 0:1] * wide).astype(BF16), (gates[:, 1:2] * wide).astype(BF16)], axis=0
        )

    def z_copy(k, i):
        dest = group_of(i)
        return remote(
            send.at[k, pl.ds(pl.multiple_of(dest * quarter, 16), quarter), :],
            rows[k].at[block(c, g), xcols], zs.at[k, i], zr.at[k, i], dest, h,
        )

    def x_copy(k, i):
        ref = rows[k].at[block(c, group_of(-i)), xcols]
        return remote(ref, ref, xs.at[k, i], xr.at[k, i], g, over)

    def c_copy(k, i):
        ref = rows[k].at[block(c, group_of(-i)), :]
        return remote(ref, ref, cs.at[k, i], cr.at[k, i], g, sib)

    others = range(1, groups)
    mine = places[pl.ds(pl.multiple_of(c * gq, 16), gq), :]
    send[0] = nn(mine[:, :tokens] + mine[:, tokens:], tok[:, xcols]).astype(BF16)
    for i in others:
        z_copy(0, i).start()
    send[1] = nn(mine, cot(xcols)).astype(BF16)
    for half in range(2):
        own = places[block(half, g), :]
        rows_x[block(half, g), :] = nn(own[:, :tokens] + own[:, tokens:], tok[...]).astype(BF16)
        for n in range(2):
            cols = slice(n * hc, n * hc + hc)
            rows_c[block(half, g), cols] = nn(own, cot(cols)).astype(BF16)

    def pass_over(k):
        for i in others:
            z_copy(k, i).wait_recv()
            x_copy(k, i).start()

    def pass_sib(k):
        for i in others:
            x_copy(k, i).wait_recv()
            c_copy(k, i).start()

    def arrived(k):
        for i in others:
            c_copy(k, i).wait_recv()

    pass_over(0)
    for i in others:
        z_copy(1, i).start()
    pass_sib(0)
    arrived(0)
    pass_over(1)

    def at_tile(n):
        return pl.ds(pl.multiple_of(n * tile, tile), tile)

    stores = []

    def store(src, dst):
        stores.append(pltpu.make_async_copy(src, dst, lsem.at[len(stores)]))
        stores[-1].start()

    loads[0].wait()
    loads[1].wait()

    @pl.loop(0, ff // tile, unroll=UNROLL)
    def _(n):
        cols = at_tile(n)
        gate = nn(rows_x[...], wg[:, cols])
        up = nn(rows_x[...], wu[:, cols])
        sigma = jax.nn.sigmoid(gate)
        act = gate * sigma
        silu[:, cols] = act
        upslope[:, cols] = up * (sigma * (1.0 + gate * (1.0 - sigma)))
        hidden[:, cols] = (act * up).astype(BF16)

    pass_sib(1)
    loads[2].wait()
    other_rows = pl.ds(pl.multiple_of((1 - c) * gq, 16), gq)

    @pl.loop(0, width // tile, unroll=UNROLL)
    def _(n):
        cols = at_tile(n)
        acc[0, :, cols] = nn(hidden[...], wd[:, cols])
        pair_send[0, :, cols] = acc[0, other_rows, cols].astype(BF16)

    def part(group):
        return pl.ds(pl.multiple_of(group * quarter, 16), quarter)

    def pair_copy(k, i, n):
        at_, cols = part(group_of(i)), (ocols, xcols)[n]
        j = i + n * groups
        return remote(
            pair_send.at[k, at_, cols], pair_recv.at[k, at_, cols],
            c2s.at[k, j], c2r.at[k, j], g, sib,
        )

    def cross_copy(k, i):
        at_ = part(group_of(i))
        return remote(
            x_send.at[k, at_, :], x_recv.at[k, at_, :], x2s.at[k, i], x2r.at[k, i], g, over
        )

    def home_copy(k, i):
        dest = group_of(i)
        return remote(
            z_send.at[k, part(dest), :], home.at[k, block(c, g), :],
            z2s.at[k, i], z2r.at[k, i], dest, h,
        )

    def twin_copy(k, i):
        ref = home.at[k, block(c, group_of(-i)), :]
        return remote(ref, ref, h2s.at[k, i], h2r.at[k, i], g, sib)

    order = list(others) + [0]

    def start_pair(k, n):
        for i in order:
            pair_copy(k, i, n).start()

    def cross(k):
        for i in order:
            pair_copy(k, i, 0).wait_recv()
            here, there = block(c, group_of(i)), part(group_of(i))
            x_send[k, there, :] = (
                acc[k, here, ocols] + pair_recv[k, there, ocols].astype(F32)
            ).astype(BF16)
            cross_copy(k, i).start()

    def go_home(k):
        for i in order:
            pair_copy(k, i, 1).wait_recv()
            cross_copy(k, i).wait_recv()
            here, there = block(c, group_of(i)), part(group_of(i))
            total = (
                (acc[k, here, xcols] + pair_recv[k, there, xcols].astype(F32))
                + x_recv[k, there, :].astype(F32)
            ).astype(BF16)
            if i == 0:
                home[k, here, :] = total
                twin_copy(k, 0).start()
            else:
                z_send[k, there, :] = total
                home_copy(k, i).start()

    def twin(k):
        for i in others:
            home_copy(k, i).wait_recv()
            twin_copy(k, i).start()

    def out_copy(k):
        return remote(
            out_send.at[k], out_full.at[k, :, xcols], os_.at[k], or_.at[k], g, over
        )

    def combine(k):
        for i in order:
            twin_copy(k, i).wait_recv()
        for to in (1 - x, x):
            base = pl.multiple_of(to * (2 * share) + c * share, 16)
            first = picks[pl.ds(base, share), :]
            second = picks[pl.ds(base + tokens, share), :]
            if k == 0:
                w = gates[pl.ds(base, share), :]
                value = w[:, 0:1] * nn(first, home[0]) + w[:, 1:2] * nn(second, home[0])
            else:
                value = nn(first + second, home[1])
            if to is x:
                out_full[k, :, xcols] = value.astype(BF16)
            else:
                out_send[k] = value.astype(BF16)
                out_copy(k).start()

    start_pair(0, 0)
    start_pair(0, 1)
    arrived(1)
    store(rows_c, c_any)

    def back_tiles(first, last):
        @pl.loop(first, last, unroll=UNROLL)
        def _(n):
            cols = at_tile(n)
            back = nt(rows_c[...], wd[cols, :])
            gpg[:, cols] = (back * upslope[:, cols]).astype(BF16)
            gpu[:, cols] = (back * silu[:, cols]).astype(BF16)

    tiles = ff // tile
    back_tiles(0, tiles // 2)
    cross(0)
    back_tiles(tiles // 2, tiles)
    store(gpg, gpg_any)
    store(gpu, gpu_any)

    def grad_cols(cols):
        acc[1, :, cols] = nt(gpg[...], wg[cols, :]) + nt(gpu[...], wu[cols, :])
        pair_send[1, :, cols] = acc[1, other_rows, cols].astype(BF16)

    for n, side in enumerate((1 - x, x)):

        @pl.loop(0, hc // tile, unroll=UNROLL)
        def _(j):
            grad_cols(pl.ds(pl.multiple_of(side * hc + j * tile, 128), tile))

        rest = hc % tile
        if rest:
            grad_cols(pl.ds(pl.multiple_of(side * hc + hc - rest, 128), rest))
        start_pair(1, n)

    cross(1)
    go_home(0)

    @pl.loop(0, width // tile)
    def _(n):
        rows_xt[at_tile(n), :] = rows_x[:, at_tile(n)].T

    store(rows_xt, xt_any)
    go_home(1)

    @pl.loop(0, tiles)
    def _(n):
        hidden_t[at_tile(n), :] = hidden[:, at_tile(n)].T

    store(hidden_t, hidt_any)
    twin(0)
    combine(0)
    twin(1)
    combine(1)
    for k in range(2):
        out_copy(k).wait_recv()
    mixed_out[...] = out_full[0]
    gtok_out[...] = out_full[1]

    for k in range(2):
        for i in others:
            z_copy(k, i).wait_send()
            x_copy(k, i).wait_send()
            c_copy(k, i).wait_send()
            home_copy(k, i).wait_send()
        for i in order:
            pair_copy(k, i, 0).wait_send()
            pair_copy(k, i, 1).wait_send()
            cross_copy(k, i).wait_send()
            twin_copy(k, i).wait_send()
        out_copy(k).wait_send()
    for s in stores:
        s.wait()


def weights_kernel(
    rows_xt, hidden_t, gpg, gpu, rows_c, mixed, gtok,
    mixed_out, gtok_out, grad_gate, grad_up, grad_down,
):
    @pl.when(pl.program_id(0) == 0)
    def _():
        mixed_out[...] = mixed[...]
        gtok_out[...] = gtok[...]

    for left, right, out in (
        (rows_xt, gpg, grad_gate),
        (rows_xt, gpu, grad_up),
        (hidden_t, rows_c, grad_down),
    ):
        piece = 768 if left.shape[0] % 768 == 0 else 256
        for m in range(0, left.shape[0], piece):
            at = slice(m, m + piece)
            out[at, :] = nn(left[at, :], right[...]).astype(BF16)


def fits(tokens, capacity, shares, width, ff):
    return (
        shares == 4
        and capacity % 32 == 0
        and tokens % 64 == 0
        and width % 256 == 0
        and ff % 256 == 0
    )


def local_fused(tokens, routes, gates, grad_out, w_gate, w_up, w_down):
    groups = lax.axis_size("grp")
    tok_rows, width = tokens.shape
    ff = w_gate.shape[2]
    capacity = capacity_of(tok_rows, routes.shape[1], groups)
    quarter = capacity // 2
    tile = 256
    rows = groups * capacity
    half_rows, hc = rows // 2, width // 2
    share = tok_rows // 4
    vmem = pl.BlockSpec(memory_space=pltpu.VMEM)
    hbm = pl.BlockSpec(memory_space=pl.ANY)
    dma = pltpu.SemaphoreType.DMA
    flops = 2 * rows * width * ff * 6
    rows_xt, rows_c, hidden_t, gpg, gpu, mixed, grad_tokens = pl.pallas_call(
        functools.partial(layer_kernel, groups, quarter, tile),
        out_shape=[
            jax.ShapeDtypeStruct((width, rows), BF16),
            jax.ShapeDtypeStruct((rows, width), BF16),
            jax.ShapeDtypeStruct((ff, rows), BF16),
            jax.ShapeDtypeStruct((rows, ff), BF16),
            jax.ShapeDtypeStruct((rows, ff), BF16),
            jax.ShapeDtypeStruct((share, width), BF16),
            jax.ShapeDtypeStruct((share, width), BF16),
        ],
        in_specs=[vmem] * 4 + [hbm] * 3,
        out_specs=[hbm] * 5 + [vmem] * 2,
        scratch_shapes=[
            pltpu.VMEM((width, ff), BF16),
            pltpu.VMEM((width, ff), BF16),
            pltpu.VMEM((ff, width), BF16),
            pltpu.VMEM((rows, width), BF16),
            pltpu.VMEM((rows, width), BF16),
            pltpu.VMEM((2, half_rows, hc), BF16),
            pltpu.VMEM((rows, 2 * tok_rows), BF16),
            pltpu.VMEM((2 * tok_rows, rows), BF16),
            pltpu.VMEM((rows, ff), F32),
            pltpu.VMEM((rows, ff), F32),
            pltpu.VMEM((rows, ff), BF16),
            pltpu.VMEM((rows, ff), BF16),
            pltpu.VMEM((rows, ff), BF16),
            pltpu.VMEM((width, rows), BF16),
            pltpu.VMEM((ff, rows), BF16),
            pltpu.VMEM((tok_rows, 2), F32),
            pltpu.VMEM((2, rows, width), F32),
            pltpu.VMEM((2, half_rows, width), BF16),
            pltpu.VMEM((2, half_rows, width), BF16),
            pltpu.VMEM((2, half_rows, hc), BF16),
            pltpu.VMEM((2, half_rows, hc), BF16),
            pltpu.VMEM((2, half_rows, hc), BF16),
            pltpu.VMEM((2, rows, hc), BF16),
            pltpu.VMEM((2, share, hc), BF16),
            pltpu.VMEM((2, share, width), BF16),
        ]
        + [dma((2, groups))] * 6
        + [dma((2, 2 * groups))] * 2
        + [dma((2, groups))] * 6
        + [dma((2,)), dma((2,)), dma((3,)), dma((5,))],
        compiler_params=pltpu.CompilerParams(
            collective_id=0, has_side_effects=True, vmem_limit_bytes=56 * 1024 * 1024
        ),
        cost_estimate=pl.CostEstimate(
            flops=flops, bytes_accessed=6 * width * ff, transcendentals=rows * ff
        ),
    )(tokens, routes.T, gates.T, grad_out, w_gate[0], w_up[0], w_down[0])
    steps = 6 if ff % 768 == 0 and width % 768 == 0 else 2
    wide, narrow = width // steps, ff // steps
    whole = lambda shape: pl.BlockSpec(shape, lambda n: (0, 0))
    side = lambda shape: pl.BlockSpec(shape, lambda n: (0, n))
    mixed, grad_tokens, grad_gate, grad_up, grad_down = pl.pallas_call(
        weights_kernel,
        grid=(steps,),
        out_shape=[
            jax.ShapeDtypeStruct((share, width), BF16),
            jax.ShapeDtypeStruct((share, width), BF16),
            jax.ShapeDtypeStruct((width, ff), BF16),
            jax.ShapeDtypeStruct((width, ff), BF16),
            jax.ShapeDtypeStruct((ff, width), BF16),
        ],
        in_specs=[
            whole((width, rows)),
            whole((ff, rows)),
            side((rows, narrow)),
            side((rows, narrow)),
            side((rows, wide)),
            whole((share, width)),
            whole((share, width)),
        ],
        out_specs=[
            whole((share, width)),
            whole((share, width)),
            side((width, narrow)),
            side((width, narrow)),
            side((ff, wide)),
        ],
        compiler_params=pltpu.CompilerParams(vmem_limit_bytes=60 * 1024 * 1024),
        cost_estimate=pl.CostEstimate(
            flops=flops // 2, bytes_accessed=6 * width * ff, transcendentals=0
        ),
    )(rows_xt, hidden_t, gpg, gpu, rows_c, mixed, grad_tokens)
    return (mixed, grad_tokens, grad_gate[None], grad_up[None], grad_down[None])


def capacity_of(tok_rows, top_count, groups):
    return max(3 * tok_rows // 8, top_count * tok_rows // groups)


def slot_numbers(route_blocks, expert_count):
    onehot = (route_blocks[..., None] == jnp.arange(expert_count, dtype=jnp.int32)).astype(
        jnp.int32
    )
    earlier = jnp.cumsum(onehot, axis=-2) - onehot
    return jnp.sum(earlier * onehot, axis=-1)


def forward_rows(rows_x, weight_gate, weight_up, weight_down):
    gate_pre = jnp.dot(rows_x, weight_gate, preferred_element_type=jnp.float32)
    up_pre = jnp.dot(rows_x, weight_up, preferred_element_type=jnp.float32)
    sigma_gate = jax.nn.sigmoid(gate_pre)
    silu_gate = gate_pre * sigma_gate
    hidden = (silu_gate * up_pre).astype(jnp.bfloat16)
    expert_out = jnp.dot(hidden, weight_down, preferred_element_type=jnp.float32)
    return (gate_pre, up_pre, sigma_gate, silu_gate, hidden, expert_out)


def backward_rows(rows_x, rows_c, weight_gate, weight_up, weight_down, saved):
    gate_pre, up_pre, sigma_gate, silu_gate, hidden, expert_out = saved
    grad_hidden = jnp.dot(rows_c, weight_down.T, preferred_element_type=jnp.float32)
    slope = sigma_gate * (1.0 + gate_pre * (1.0 - sigma_gate))
    grad_pre_gate = (grad_hidden * up_pre * slope).astype(jnp.bfloat16)
    grad_pre_up = (grad_hidden * silu_gate).astype(jnp.bfloat16)
    grad_rows = jnp.dot(grad_pre_gate, weight_gate.T, preferred_element_type=jnp.float32)
    grad_rows = grad_rows + jnp.dot(grad_pre_up, weight_up.T, preferred_element_type=jnp.float32)
    grad_wgate = jnp.dot(rows_x.T, grad_pre_gate, preferred_element_type=jnp.float32).astype(
        jnp.bfloat16
    )
    grad_wup = jnp.dot(rows_x.T, grad_pre_up, preferred_element_type=jnp.float32).astype(
        jnp.bfloat16
    )
    grad_wdown = jnp.dot(hidden.T, rows_c, preferred_element_type=jnp.float32).astype(jnp.bfloat16)
    return (grad_rows, grad_wgate, grad_wup, grad_wdown)


def combine_pairs(whole, weights, row_ids):
    members, groups, capacity, width = whole.shape
    tok_count, top_count = row_ids.shape
    flat = whole.reshape(members, groups * capacity, width)
    picked = jnp.take(flat, row_ids.reshape(-1), axis=1).reshape(
        members, tok_count, top_count, width
    )
    return jnp.sum(weights[..., None] * picked, axis=2)


def send_back(stacked, weights, target_row):
    shares = lax.axis_size("hid")
    share = lax.axis_index("hid")
    tok_rows, top_count = target_row.shape
    summed = lax.psum_scatter(stacked, "hid", scatter_dimension=2, tiled=True)
    moved = lax.all_to_all(summed, "grp", split_axis=1, concat_axis=1, tiled=True)
    whole = lax.all_gather(moved, "hid", axis=2, tiled=True)
    own_count = tok_rows // shares
    own_rows = lax.dynamic_slice_in_dim(target_row, share * own_count, own_count, 0)
    own_weights = lax.dynamic_slice_in_dim(weights, share * own_count, own_count, 1)
    return combine_pairs(whole, own_weights, own_rows)


def local_plain(tokens, routes, gates, grad_out, w_gate, w_up, w_down):
    groups = lax.axis_size("grp")
    shares = lax.axis_size("hid")
    share = lax.axis_index("hid")
    tok_rows, width = tokens.shape
    top_count = routes.shape[1]
    capacity = max(3 * tok_rows // 8, top_count * tok_rows // groups)
    part_slots = capacity // shares
    pairs = tok_rows * top_count
    flat_routes = routes.T.reshape(pairs)
    slot_index = slot_numbers(flat_routes[None, :], groups)[0]
    target_row = flat_routes * capacity + slot_index
    wanted = (
        jnp.arange(groups, dtype=jnp.int32)[:, None] * capacity
        + share * part_slots
        + jnp.arange(part_slots, dtype=jnp.int32)[None, :]
    ).reshape(-1)
    placer = (wanted[:, None] == target_row[None, :]).astype(jnp.bfloat16)
    tok_pairs = jnp.tile(tokens, (top_count, 1))
    cot_pairs = (
        gates.T.reshape(pairs, 1) * jnp.tile(grad_out, (top_count, 1)).astype(jnp.float32)
    ).astype(jnp.bfloat16)
    send_x = (
        jnp.dot(placer, tok_pairs, preferred_element_type=jnp.float32)
        .astype(jnp.bfloat16)
        .reshape(groups, part_slots, width)
    )
    send_c = (
        jnp.dot(placer, cot_pairs, preferred_element_type=jnp.float32)
        .astype(jnp.bfloat16)
        .reshape(groups, part_slots, width)
    )
    arrived = (
        lax.all_to_all(send_x, "grp", split_axis=0, concat_axis=0, tiled=True),
        lax.all_to_all(send_c, "grp", split_axis=0, concat_axis=0, tiled=True),
    )
    block_x, block_c = (
        lax.all_gather(arrived[0], "hid", axis=1, tiled=True),
        lax.all_gather(arrived[1], "hid", axis=1, tiled=True),
    )
    block_shape = block_x.shape
    rows_x = block_x.reshape(-1, width)
    rows_c = block_c.reshape(-1, width)
    weight_gate = w_gate[0]
    weight_up = w_up[0]
    weight_down = w_down[0]
    row_table = target_row.reshape(top_count, tok_rows).T
    plain = jnp.ones_like(gates)
    saved = forward_rows(rows_x, weight_gate, weight_up, weight_down)
    out_terms = saved[5].reshape(block_shape)
    grad_rows, grad_wgate, grad_wup, grad_wdown = backward_rows(
        rows_x, rows_c, weight_gate, weight_up, weight_down, saved
    )
    home_both = send_back(
        jnp.stack([out_terms, grad_rows.reshape(block_shape)]), jnp.stack([gates, plain]), row_table
    )
    home_out = home_both[0]
    home_grad = home_both[1]
    mixed = home_out.astype(jnp.bfloat16)
    grad_tokens = home_grad.astype(jnp.bfloat16)
    return (mixed, grad_tokens, grad_wgate[None], grad_wup[None], grad_wdown[None])


def local(tokens, routes, gates, grad_out, w_gate, w_up, w_down):
    capacity = capacity_of(tokens.shape[0], routes.shape[1], lax.axis_size("grp"))
    args = (tokens, routes, gates, grad_out, w_gate, w_up, w_down)
    shares = lax.axis_size("hid")
    if fits(tokens.shape[0], capacity, shares, tokens.shape[1], w_gate.shape[2]):
        return local_fused(*args)
    return local_plain(*args)


def solution(mesh):
    in_specs = (
        P(("rep", "grp"), None),
        P(("rep", "grp"), None),
        P(("rep", "grp"), None),
        P(("rep", "grp"), None),
        P("grp", None, "hid"),
        P("grp", None, "hid"),
        P("grp", "hid", None),
    )
    out_specs = (
        P(("rep", "grp", "hid"), None),
        P(("rep", "grp", "hid"), None),
        P(("rep", "grp"), None, "hid"),
        P(("rep", "grp"), None, "hid"),
        P(("rep", "grp"), "hid", None),
    )
    return jax.shard_map(local, mesh=mesh, in_specs=in_specs, out_specs=out_specs, check_vma=False)
```
